32 devices in a mesh: group: 2 (over x), row: 8 (over z, y), rhs: 2 (over core).
Axes of the slice: x: 2, y: 2, z: 4, core: 2. Of those that a mesh axis runs over, the one named last changes fastest.
Arguments:
- u_panels: float32 [8192, 1536], P(('group', 'row')), parts along dimension 0, may hold values from -0.078125 to 0.078125
- u_diag: float32 [3072], P('group'), parts along dimension 0, may hold values from 0.5 to 2
- l_panels: float32 [8192, 1536], P(('group', 'row')), parts along dimension 0, may hold values from -0.078125 to 0.078125
- right_side: float32 [8192, 512], P(('group', 'row'), 'rhs'), parts along dimension 0, may hold values from -6 to 6
- x_tail: float32 [8192, 512], P(('group', 'row'), 'rhs'), parts along dimension 0, may hold values from -6 to 6
- slot_blocks: int32 [16], P('group'), parts along dimension 0, may hold values from 0 to 7, as said below
Outputs:
- forward_out: float32 [8192, 512], P(('group', 'row'), 'rhs'), parts along dimension 0
- solution: float32 [8192, 512], P(('group', 'row'), 'rhs'), parts along dimension 0
The draws below stay inside these ranges and needn't reach their ends.
There are 2 independent parts, one for each index of `group`. The reference program is written for one: setup_inputs(seed, part) draws one part's arguments, and reference() takes and returns one part's arrays. A program takes and returns all parts, laid end to end along the dimension named above; each array names one. Nothing has to cross between parts.
Inputs may be any that keep to these rules, and one draw needn't show every extreme that they name: `slot_blocks`: a permutation of the 8 global row blocks, each named once.
All inputs are finite; a program needn't handle non-finite values.
Results may differ from the reference program's by a relative error of at most 0.000065.
Values sent between devices are 32-bit elements; how exact they have to be, the bound alone decides.
A program may use at most 64 MiB of HBM per device.

```python
import math
import jax
import jax.numpy as jnp
from jax import lax

PANEL = 512
PANELS = 3
BLOCKS = 8
RHS = 512


def draw_slot_blocks(key, part):
    return jax.random.permutation(key, BLOCKS).astype(jnp.int32)


def shard_levels(stream_key, shape, shards, low, largest):
    loudness, own = 1.0, jax.random.fold_in(stream_key, 6)
    for dim, blocks in shards:
        steps = jnp.exp(jax.random.uniform(jax.random.fold_in(own, dim), (blocks,), jnp.float32, low / len(shards), largest / len(shards)))
        loudness = loudness * jnp.repeat(steps, shape[dim] // blocks).reshape([-1 if axis == dim else 1 for axis in range(len(shape))])
    return loudness


def gaussian(own_key, dims, width, most, pieces=(), held_as=jnp.bfloat16):
    values = width * jax.random.normal(own_key, dims, jnp.float32)
    if pieces:
        values = values * shard_levels(own_key, dims, pieces, -0.22, 0.18)
    return jnp.clip(values, -most, most).astype(held_as)


def setup_inputs(seed: int = 0, part: int = 0) -> dict:
    key_list = jax.random.split(jax.random.key(seed), 7)
    own_keys = jax.random.split(jax.random.fold_in(key_list[6], part), 7)
    return {
        "u_panels": gaussian(own_keys[0], (BLOCKS * PANEL, PANELS * PANEL), (4 * PANELS * PANEL) ** -0.5, 0.078125, ((0, 8),), jnp.float32),
        "u_diag": jnp.clip(jnp.exp(jax.random.uniform(own_keys[1], (PANELS * PANEL,), jnp.float32, math.log(0.5), math.log(2.0))), 0.5, 2.0),
        "l_panels": gaussian(own_keys[2], (BLOCKS * PANEL, PANELS * PANEL), (4 * PANELS * PANEL) ** -0.5, 0.078125, ((0, 8),), jnp.float32),
        "right_side": gaussian(own_keys[3], (BLOCKS * PANEL, RHS), 1.0, 6.0, ((0, 8), (1, 2)), jnp.float32),
        "x_tail": gaussian(own_keys[4], (BLOCKS * PANEL, RHS), 1.0, 6.0, ((0, 8), (1, 2)), jnp.float32),
        "slot_blocks": draw_slot_blocks(jax.random.fold_in(jax.random.fold_in(key_list[6], part), 71), part),
    }


def to_global(stored, slot_blocks):
    shaped = stored.reshape((BLOCKS, PANEL) + stored.shape[1:])
    placed = jnp.zeros_like(shaped).at[slot_blocks].set(shaped)
    return placed.reshape(stored.shape)

def to_stored(whole, slot_blocks):
    shaped = whole.reshape((BLOCKS, PANEL) + whole.shape[1:])
    return shaped[slot_blocks].reshape(whole.shape)

def reference(u_panels, u_diag, l_panels, right_side, x_tail, slot_blocks):
    head = PANELS * PANEL
    total_rows = BLOCKS * PANEL
    row_ids = lax.broadcasted_iota(jnp.int32, (total_rows, head), 0)
    col_ids = lax.broadcasted_iota(jnp.int32, (total_rows, head), 1)
    strict = row_ids > col_ids
    upper_low = jnp.where(strict, to_global(u_panels, slot_blocks), 0.0)
    lower_low = jnp.where(strict, to_global(l_panels, slot_blocks), 0.0)
    rhs_global = to_global(right_side, slot_blocks)
    tail_global = to_global(x_tail, slot_blocks)
    head_upper = upper_low[:head] + jnp.diag(u_diag)
    forward_head = lax.linalg.triangular_solve(head_upper, rhs_global[:head], left_side=True, lower=True)
    forward_tail = rhs_global[head:] - jnp.dot(upper_low[head:].astype(jnp.float32), forward_head.astype(jnp.float32), precision=lax.Precision.HIGHEST, preferred_element_type=jnp.float32)
    forward_all = jnp.concatenate([forward_head, forward_tail], axis=0)
    coupled = lax.dot_general(lower_low[head:].astype(jnp.float32), tail_global[head:].astype(jnp.float32), (((0,), (0,)), ((), ())), precision=lax.Precision.HIGHEST, preferred_element_type=jnp.float32)
    solution_head = lax.linalg.triangular_solve(lower_low[:head], forward_head - coupled, left_side=True, lower=True, transpose_a=True, unit_diagonal=True)
    solution_all = jnp.concatenate([solution_head, tail_global[head:]], axis=0)
    return (to_stored(forward_all, slot_blocks), to_stored(solution_all, slot_blocks))
```

```python
import functools

import jax
import jax.numpy as jnp
from jax import lax
from jax.experimental import pallas as pl
from jax.experimental.pallas import tpu as pltpu
from jax.sharding import PartitionSpec as P

PANEL = 512
PANELS = 3
TILE = 128
BASE = 16
F32 = jnp.float32
NN = (((1,), (0,)), ((), ()))
TN = (((0,), (0,)), ((), ()))


def split(value):
    high = value.astype(jnp.bfloat16)
    return high, (value - high.astype(F32)).astype(jnp.bfloat16)


def dot3(left, right, dims=NN):
    lh, ll = split(left)
    rh, rl = split(right)
    dot = functools.partial(lax.dot_general, dimension_numbers=dims, preferred_element_type=F32)
    return dot(lh, rh) + (dot(lh, rl) + dot(ll, rh))


def unit_inverse(strict):
    size = strict.shape[0]
    row = lax.broadcasted_iota(jnp.int32, (TILE, TILE), 0)
    col = lax.broadcasted_iota(jnp.int32, (TILE, TILE), 1)
    eye = jnp.where(row == col, 1.0, 0.0)
    done = []
    for start in range(0, size, TILE):
        tile = strict[start : start + TILE, start : start + TILE]
        power = jnp.where(row // BASE == col // BASE, tile, 0.0)
        inverse = eye - power
        order = 2
        while order < BASE:
            power = dot3(power, power)
            inverse = inverse + dot3(inverse, power)
            order *= 2
        block = BASE
        while block < TILE:
            off = jnp.where(
                (row // (2 * block) == col // (2 * block)) & (row // block != col // block), tile, 0.0
            )
            inverse = inverse - dot3(inverse, dot3(off, inverse))
            block *= 2
        done.append(inverse)
    block = TILE
    while block < size:
        merged = []
        for index in range(0, len(done), 2):
            start = index * block
            off = strict[start + block : start + 2 * block, start : start + block]
            corner = -dot3(done[index + 1], dot3(off, done[index]))
            top = jnp.concatenate([done[index], jnp.zeros_like(corner)], axis=1)
            merged.append(jnp.concatenate([top, jnp.concatenate([corner, done[index + 1]], axis=1)], axis=0))
        done = merged
        block *= 2
    return done[0]


def strictly_lower(block):
    row = lax.broadcasted_iota(jnp.int32, block.shape, 0)
    col = lax.broadcasted_iota(jnp.int32, block.shape, 1)
    return jnp.where(row > col, block, 0.0)


def upper_start(place, panel, diag, rhs, inverse, first):
    mine = place[1]
    inverse[...] = jnp.zeros_like(inverse)
    first[...] = jnp.zeros_like(first)

    @pl.when(mine < PANELS)
    def _():
        row = lax.broadcasted_iota(jnp.int32, (TILE, TILE), 0)
        col = lax.broadcasted_iota(jnp.int32, (TILE, TILE), 1)
        across = diag[0]
        down = jnp.concatenate(
            [
                jnp.sum(
                    jnp.where(row == col, across[:, start : start + TILE], 0.0), axis=1, keepdims=True
                )
                for start in range(0, PANEL, TILE)
            ],
            axis=0,
        )
        strict = strictly_lower(panel[...]) / down
        inverse[...] = unit_inverse(strict) / across

    @pl.when(mine == 0)
    def _():
        first[...] = dot3(inverse[...], rhs[...])


def lower_start(place, diag_panel, panel, tail, inverse, partial):
    mine = place[1]

    @pl.when(mine < PANELS)
    def _():
        inverse[...] = unit_inverse(strictly_lower(diag_panel[...])).T
        partial[...] = jnp.zeros_like(partial)

    @pl.when(mine >= PANELS)
    def _():
        inverse[...] = jnp.zeros_like(inverse)
        partial[...] = dot3(panel[...], tail[...], TN)


def tail_product(place, panel, tail, partial):
    mine = place[1]
    partial[...] = jnp.zeros_like(partial)

    @pl.when(mine >= PANELS)
    def _():
        partial[...] = dot3(panel[...], tail[...], TN)


def forward_step(index, place, panel, inverse, values, state, after, candidate):
    mine = place[1]
    after[...] = state[...]

    @pl.when(mine > index)
    def _():
        after[...] = state[...] - dot3(panel[...], values[...])

    @pl.when(mine == index)
    def _():
        after[...] = values[...]

    candidate[...] = jnp.zeros_like(candidate)

    @pl.when(mine == index + 1)
    def _():
        candidate[...] = dot3(inverse[...], after[...])


def last_forward(place, panel, inverse, values, state, lower_inverse, below, partial, summed, after, candidate, solved, sent):
    mine = place[1]
    last = PANELS - 1
    after[...] = state[...]
    candidate[...] = jnp.zeros_like(candidate)
    solved[...] = jnp.zeros_like(solved)
    sent[...] = partial[...]

    @pl.when(mine > last - 1)
    def _():
        after[...] = state[...] - dot3(panel[...], values[...])

    @pl.when(mine == last - 1)
    def _():
        after[...] = values[...]

    @pl.when(mine == last)
    def _():
        candidate[...] = dot3(inverse[...], after[...])
        solved[...] = dot3(lower_inverse[...], candidate[...] - summed[...])
        sent[...] = dot3(below[...], solved[...], TN)


def backward_step(index, place, inverse, forward, summed, partial, result, below, solved, sent):
    mine = place[1]
    solved[...] = result[...]
    sent[...] = partial[...]

    @pl.when(mine == index)
    def _():
        solved[...] = dot3(inverse[...], forward[...] - summed[...])
        sent[...] = dot3(below[...], solved[...], TN)


def backward_last(place, inverse, forward, summed, result, tail, solved):
    mine = place[1]
    solved[...] = result[...]

    @pl.when(mine == 0)
    def _():
        solved[...] = dot3(inverse[...], forward[...] - summed[...])

    @pl.when(mine >= PANELS)
    def _():
        solved[...] = tail[...]


def forward_end(place, panel, values, state, after):
    mine = place[1]
    after[...] = state[...]

    @pl.when(mine >= PANELS)
    def _():
        after[...] = state[...] - dot3(panel[...], values[...])

    @pl.when(mine == PANELS - 1)
    def _():
        after[...] = values[...]


def full(shape):
    return pl.BlockSpec(shape, lambda step, place: (0,) * len(shape))


def columns(index, width=1):
    return pl.BlockSpec((PANEL, width * PANEL), lambda step, place: (0, index))


OWN = pl.BlockSpec((PANEL, PANEL), lambda step, place: (0, place[0]))


def call(kernel, place, ins, outs):
    arrays = [array for array, _ in ins]
    specs = [full(array.shape) if spec is None else spec for array, spec in ins]
    return pl.pallas_call(
        kernel,
        grid_spec=pltpu.PrefetchScalarGridSpec(
            num_scalar_prefetch=1,
            grid=(1,),
            in_specs=specs,
            out_specs=[full(shape) for shape in outs],
        ),
        out_shape=[jax.ShapeDtypeStruct(shape, F32) for shape in outs],
        compiler_params=pltpu.CompilerParams(vmem_limit_bytes=40 * 1024 * 1024),
    )(place, *arrays)


def body(u_panels, u_diag, l_panels, right_side, x_tail, slot_blocks):
    width = right_side.shape[1]
    mine = slot_blocks[lax.axis_index("row")]
    place = jnp.stack([jnp.minimum(mine, PANELS - 1), mine]).astype(jnp.int32)
    square, block = (PANEL, PANEL), (PANEL, width)
    diag = u_diag.reshape(PANELS, 1, PANEL)
    last = PANELS - 1
    total = lambda value: lax.psum(value, "row")

    (part2,) = call(tail_product, place, [(l_panels, columns(last)), (x_tail, None)], [block])
    sum2 = total(part2)
    upper_inv, first = call(
        upper_start,
        place,
        [
            (u_panels, OWN),
            (diag, pl.BlockSpec((1, 1, PANEL), lambda step, place: (place[0], 0, 0))),
            (right_side, None),
        ],
        [square, block],
    )
    y0 = total(first)
    lower_inv, part01 = call(
        lower_start,
        place,
        [(l_panels, OWN), (l_panels, columns(0, last)), (x_tail, None)],
        [square, (last * PANEL, width)],
    )
    state, second = call(
        functools.partial(forward_step, 0),
        place,
        [(u_panels, columns(0)), (upper_inv, None), (y0, None), (right_side, None)],
        [block, block],
    )
    y1 = total(second)
    state, third, result, sent = call(
        last_forward,
        place,
        [
            (u_panels, columns(1)),
            (upper_inv, None),
            (y1, None),
            (state, None),
            (lower_inv, None),
            (l_panels, columns(0, last)),
            (part01, None),
            (sum2, None),
        ],
        [block, block, block, (last * PANEL, width)],
    )
    sum1 = total(sent[PANEL:])
    third, sum1 = lax.optimization_barrier((third, sum1))
    result, sent0 = call(
        functools.partial(backward_step, 1),
        place,
        [
            (lower_inv, None),
            (y1, None),
            (sum1, None),
            (sent[:PANEL], None),
            (result, None),
            (l_panels, columns(0)),
        ],
        [block, block],
    )
    sum0 = total(sent0)
    y2 = total(third)
    (forward_out,) = call(
        forward_end, place, [(u_panels, columns(last)), (y2, None), (state, None)], [block]
    )
    (solution_out,) = call(
        backward_last,
        place,
        [(lower_inv, None), (y0, None), (sum0, None), (result, None), (x_tail, None)],
        [block],
    )
    return (forward_out, solution_out)


def solution(mesh):
    placed = (
        P(("group", "row"), None),
        P("group"),
        P(("group", "row"), None),
        P(("group", "row"), "rhs"),
        P(("group", "row"), "rhs"),
        P("group"),
    )
    return jax.shard_map(
        body,
        mesh=mesh,
        in_specs=placed,
        out_specs=(P(("group", "row"), "rhs"), P(("group", "row"), "rhs")),
        check_vma=False,
    )
```

```python
import functools

import jax
import jax.numpy as jnp
from jax import lax
from jax.experimental import pallas as pl
from jax.experimental.pallas import tpu as pltpu
from jax.sharding import PartitionSpec as P

PANEL = 512
PANELS = 3
TILE = 128
BASE = 16
F32 = jnp.float32
NN = (((1,), (0,)), ((), ()))
TN = (((0,), (0,)), ((), ()))


def split(value):
    high = value.astype(jnp.bfloat16)
    return high, (value - high.astype(F32)).astype(jnp.bfloat16)


def dot3(left, right, dims=NN):
    lh, ll = split(left)
    rh, rl = split(right)
    dot = functools.partial(lax.dot_general, dimension_numbers=dims, preferred_element_type=F32)
    return dot(lh, rh) + (dot(lh, rl) + dot(ll, rh))


def unit_inverse(strict):
    size = strict.shape[0]
    row = lax.broadcasted_iota(jnp.int32, (TILE, TILE), 0)
    col = lax.broadcasted_iota(jnp.int32, (TILE, TILE), 1)
    eye = jnp.where(row == col, 1.0, 0.0)
    done = []
    for start in range(0, size, TILE):
        tile = strict[start : start + TILE, start : start + TILE]
        power = jnp.where(row // BASE == col // BASE, tile, 0.0)
        inverse = eye - power
        order = 2
        while order < BASE:
            power = dot3(power, power)
            inverse = inverse + dot3(inverse, power)
            order *= 2
        block = BASE
        while block < TILE:
            off = jnp.where(
                (row // (2 * block) == col // (2 * block)) & (row // block != col // block), tile, 0.0
            )
            inverse = inverse - dot3(inverse, dot3(off, inverse))
            block *= 2
        done.append(inverse)
    block = TILE
    while block < size:
        merged = []
        for index in range(0, len(done), 2):
            start = index * block
            off = strict[start + block : start + 2 * block, start : start + block]
            corner = -dot3(done[index + 1], dot3(off, done[index]))
            top = jnp.concatenate([done[index], jnp.zeros_like(corner)], axis=1)
            merged.append(jnp.concatenate([top, jnp.concatenate([corner, done[index + 1]], axis=1)], axis=0))
        done = merged
        block *= 2
    return done[0]


def strictly_lower(block):
    row = lax.broadcasted_iota(jnp.int32, block.shape, 0)
    col = lax.broadcasted_iota(jnp.int32, block.shape, 1)
    return jnp.where(row > col, block, 0.0)


def prepare(place, u_own, l_own, diag, rhs, lower, tail, upper_inv, lower_inv, first, partial):
    mine = place[1]
    first[...] = jnp.zeros_like(first)

    @pl.when(mine < PANELS)
    def _():
        row = lax.broadcasted_iota(jnp.int32, (TILE, TILE), 0)
        col = lax.broadcasted_iota(jnp.int32, (TILE, TILE), 1)
        across = diag[0]
        down = jnp.concatenate(
            [
                jnp.sum(
                    jnp.where(row == col, across[:, start : start + TILE], 0.0), axis=1, keepdims=True
                )
                for start in range(0, PANEL, TILE)
            ],
            axis=0,
        )
        upper_inv[...] = unit_inverse(strictly_lower(u_own[...]) / down) / across
        lower_inv[...] = unit_inverse(strictly_lower(l_own[...])).T
        partial[...] = jnp.zeros_like(partial)

    @pl.when(mine == 0)
    def _():
        first[...] = dot3(upper_inv[...], rhs[...])

    @pl.when(mine >= PANELS)
    def _():
        upper_inv[...] = jnp.zeros_like(upper_inv)
        lower_inv[...] = jnp.zeros_like(lower_inv)
        partial[...] = dot3(lower[...], tail[...], TN).reshape(partial.shape)


class Sum:
    def __init__(self, index, source, pair_in, held, line_in, result, sends, recvs):
        self.source, self.result = source, result
        self.pair_in, self.held, self.line_in = pair_in.at[index], held.at[index], line_in.at[index]
        self.sends, self.recvs = sends.at[index], recvs.at[index]
        self.outer = lax.axis_size("row") // 2
        self.slice = PANEL // (2 * self.outer)
        me = lax.axis_index("row")
        self.side, self.along = me % 2, me // 2
        self.partner = self.along * 2 + 1 - self.side
        self.started = []

    def rows(self, side, along):
        start = side * (PANEL // 2) + along * self.slice
        return pl.ds(pl.multiple_of(start, self.slice), self.slice)

    def peer(self, offset):
        return lax.rem(self.along + offset, self.outer)

    def before(self, offset):
        return lax.rem(self.along + self.outer - offset, self.outer)

    def send(self, stage, slot, source, target, device):
        copy = pltpu.make_async_remote_copy(
            src_ref=source,
            dst_ref=target,
            send_sem=self.sends.at[stage, slot],
            recv_sem=self.recvs.at[stage, slot],
            device_id={"row": device},
            device_id_type=pl.DeviceIdType.MESH,
        )
        copy.start()
        self.started.append(copy)
        return copy

    def order(self):
        return list(range(1, self.outer)) + [0]

    def start(self):
        self.pair = {}
        for offset in self.order():
            rows = self.rows(1 - self.side, self.peer(offset))
            self.pair[offset] = self.send(
                0, offset, self.source.at[rows], self.pair_in.at[offset], self.partner
            )

    def middle(self):
        self.line = {}
        for offset in self.order():
            self.pair[offset].wait_recv()
            rows = self.rows(self.side, self.peer(offset))
            self.held[offset] = self.source[rows, :] + self.pair_in[offset]
            if offset:
                self.line[offset] = self.send(
                    1,
                    offset,
                    self.held.at[offset],
                    self.line_in.at[offset],
                    self.peer(offset) * 2 + self.side,
                )

    def finish(self):
        whole = self.held[0]
        for offset in range(1, self.outer):
            self.line[offset].wait_recv()
            whole = whole + self.line_in[offset]
        rows = self.rows(self.side, self.along)
        self.result[rows, :] = whole
        self.back = {}
        self.last = {}
        part = self.result.at[rows]
        for offset in range(1, self.outer):
            self.back[offset] = self.send(
                2, offset, part, part, self.peer(offset) * 2 + self.side
            )
        self.last[0] = self.send(3, 0, part, part, self.partner)

    def gather(self):
        for offset in range(1, self.outer):
            self.back[offset].wait_recv()
            part = self.result.at[self.rows(self.side, self.before(offset))]
            self.last[offset] = self.send(3, offset, part, part, self.partner)

    def end(self):
        for offset in range(self.outer):
            self.last[offset].wait_recv()

    def drain(self):
        for copy in self.started:
            copy.wait_send()


def chain(
    place, upper, lower, upper_inv, lower_inv, rhs, tail, first, partial,
    forward_out, solution_out,
    y0, y1, y2, s0, s1, s2, state, held_x, c1, c2, c3, c4, pair_in, held, line_in, sends, recvs,
):
    outer = lax.axis_size("row") // 2
    me = lax.axis_index("row")
    side, along = me % 2, me // 2
    barrier = pltpu.get_barrier_semaphore()
    peers = [along * 2 + 1 - side]
    peers += [lax.rem(along + offset, outer) * 2 + side for offset in range(1, outer)]
    for peer in peers:
        pl.semaphore_signal(
            barrier, inc=1, device_id={"row": peer}, device_id_type=pl.DeviceIdType.MESH
        )
    pl.semaphore_wait(barrier, len(peers))

    mine = jnp.full(rhs.shape, place[1], jnp.int32)

    def make(index, source, result):
        return Sum(index, source, pair_in, held, line_in, result, sends, recvs)

    sum_y0 = make(0, first, y0)
    sum_c2 = make(1, partial.at[2], s2)
    sum_y0.start()
    sum_c2.start()
    sum_y0.middle()
    sum_c2.middle()
    sum_y0.finish()
    sum_y0.gather()
    sum_c2.finish()
    sum_y0.end()

    state[...] = rhs[...] - jnp.where(mine > 0, dot3(upper[:, :PANEL], y0[...]), 0.0)
    c1[...] = jnp.where(mine == 1, dot3(upper_inv[...], state[...]), 0.0)
    sum_y1 = make(2, c1, y1)
    sum_y1.start()
    sum_c2.gather()
    sum_y1.middle()
    sum_y1.finish()
    sum_y1.gather()
    sum_c2.end()
    sum_y1.end()

    state[...] = state[...] - jnp.where(mine > 1, dot3(upper[:, PANEL : 2 * PANEL], y1[...]), 0.0)
    c2[...] = jnp.where(mine == 2, dot3(upper_inv[...], state[...]), 0.0)
    held_x[...] = jnp.where(mine == 2, dot3(lower_inv[...], c2[...] - s2[...]), 0.0)
    c3[...] = partial[1] + dot3(lower[:, PANEL : 2 * PANEL], held_x[...], TN)
    sum_c1 = make(3, c3, s1)
    sum_y2 = make(4, c2, y2)
    sum_c1.start()
    sum_y2.start()
    c4[...] = partial[0] + dot3(lower[:, :PANEL], held_x[...], TN)
    sum_c1.middle()
    sum_y2.middle()
    sum_c1.finish()
    sum_c1.gather()
    sum_y2.finish()
    sum_c1.end()

    x1 = jnp.where(mine == 1, dot3(lower_inv[...], y1[...] - s1[...]), 0.0)
    held_x[...] = held_x[...] + x1
    c4[...] = c4[...] + dot3(lower[:, :PANEL], x1, TN)
    sum_c0 = make(5, c4, s0)
    sum_c0.start()
    sum_y2.gather()
    sum_c0.middle()
    sum_y2.end()
    sum_c0.finish()
    sum_c0.gather()
    past = state[...] - dot3(upper[:, 2 * PANEL :], y2[...])
    own = jnp.where(mine == 0, y0[...], jnp.where(mine == 1, y1[...], y2[...]))
    forward_out[...] = jnp.where(mine >= PANELS, past, own)
    sum_c0.end()
    x0 = dot3(lower_inv[...], y0[...] - s0[...])
    head = jnp.where(mine == 0, x0, held_x[...])
    solution_out[...] = jnp.where(mine >= PANELS, tail[...], head)
    for one in (sum_y0, sum_c2, sum_y1, sum_c1, sum_y2, sum_c0):
        one.drain()


def full(shape):
    return pl.BlockSpec(shape, lambda step, place: (0,) * len(shape))


OWN = pl.BlockSpec((PANEL, PANEL), lambda step, place: (0, place[0]))


def body(row_count, u_panels, u_diag, l_panels, right_side, x_tail, slot_blocks):
    width = right_side.shape[1]
    mine = slot_blocks[lax.axis_index("row")]
    place = jnp.stack([jnp.minimum(mine, PANELS - 1), mine]).astype(jnp.int32)
    square, block = (PANEL, PANEL), (PANEL, width)
    diag = u_diag.reshape(PANELS, 1, PANEL)
    limit = pltpu.CompilerParams(vmem_limit_bytes=40 * 1024 * 1024)
    shapes = [square, square, block, (PANELS, *block)]
    upper_inv, lower_inv, first, partial = pl.pallas_call(
        prepare,
        grid_spec=pltpu.PrefetchScalarGridSpec(
            num_scalar_prefetch=1,
            grid=(1,),
            in_specs=[
                OWN,
                OWN,
                pl.BlockSpec((1, 1, PANEL), lambda step, place: (place[0], 0, 0)),
                full(block),
                full(l_panels.shape),
                full(block),
            ],
            out_specs=[full(shape) for shape in shapes],
        ),
        out_shape=[jax.ShapeDtypeStruct(shape, F32) for shape in shapes],
        compiler_params=limit,
    )(place, u_panels, l_panels, diag, right_side, l_panels, x_tail)
    outer = row_count // 2
    piece = PANEL // row_count
    sums = 6
    vmem = pl.BlockSpec(memory_space=pltpu.VMEM)
    slots = pltpu.VMEM((sums, outer, piece, width), F32)
    return pl.pallas_call(
        chain,
        in_specs=[pl.BlockSpec(memory_space=pltpu.SMEM)] + [vmem] * 8,
        out_specs=[vmem] * 2,
        out_shape=[jax.ShapeDtypeStruct(block, F32)] * 2,
        scratch_shapes=[pltpu.VMEM(block, F32)] * 12
        + [slots] * 3
        + [pltpu.SemaphoreType.DMA((sums, 4, outer))] * 2,
        compiler_params=pltpu.CompilerParams(
            collective_id=0, has_side_effects=True, vmem_limit_bytes=48 * 1024 * 1024
        ),
    )(place, u_panels, l_panels, upper_inv, lower_inv, right_side, x_tail, first, partial)


def solution(mesh):
    placed = (
        P(("group", "row"), None),
        P("group"),
        P(("group", "row"), None),
        P(("group", "row"), "rhs"),
        P(("group", "row"), "rhs"),
        P("group"),
    )
    return jax.shard_map(
        functools.partial(body, mesh.shape["row"]),
        mesh=mesh,
        in_specs=placed,
        out_specs=(P(("group", "row"), "rhs"), P(("group", "row"), "rhs")),
        check_vma=False,
    )
```

```python
import functools

import jax
import jax.numpy as jnp
from jax import lax
from jax.experimental import pallas as pl
from jax.experimental.pallas import tpu as pltpu
from jax.sharding import PartitionSpec as P

PANEL = 512
PANELS = 3
TILE = 128
BASE = 16
F32 = jnp.float32
NN = (((1,), (0,)), ((), ()))
TN = (((0,), (0,)), ((), ()))


def split(value):
    high = value.astype(jnp.bfloat16)
    return high, (value - high.astype(F32)).astype(jnp.bfloat16)


def dot3(left, right, dims=NN):
    lh, ll = split(left)
    rh, rl = split(right)
    dot = functools.partial(lax.dot_general, dimension_numbers=dims, preferred_element_type=F32)
    return dot(lh, rh) + (dot(lh, rl) + dot(ll, rh))


def inverse_stages(part, size):
    row = lax.broadcasted_iota(jnp.int32, (TILE, TILE), 0)
    col = lax.broadcasted_iota(jnp.int32, (TILE, TILE), 1)
    eye = jnp.where(row == col, 1.0, 0.0)
    done = []
    for start in range(0, size, TILE):
        tile = part(start, start, TILE)
        power = jnp.where((row // BASE == col // BASE) & (row > col), tile, 0.0)
        inverse = eye - power
        order = 2
        while order < BASE:
            power = dot3(power, power)
            inverse = inverse + dot3(inverse, power)
            order *= 2
        block = BASE
        while block < TILE:
            off = jnp.where(
                (row // (2 * block) == col // (2 * block)) & (row // block > col // block), tile, 0.0
            )
            inverse = inverse - dot3(inverse, dot3(off, inverse))
            block *= 2
        done.append(inverse)
        if start % (2 * TILE):
            yield None
    block = TILE
    while block < size:
        merged = []
        for index in range(0, len(done), 2):
            start = index * block
            off = part(start + block, start, block)
            corner = -dot3(done[index + 1], dot3(off, done[index]))
            top = jnp.concatenate([done[index], jnp.zeros_like(corner)], axis=1)
            merged.append(jnp.concatenate([top, jnp.concatenate([corner, done[index + 1]], axis=1)], axis=0))
        done = merged
        block *= 2
    yield done[0]


class Sum:
    def __init__(self, index, source, pair_in, held, line_in, result, sends, recvs):
        self.source, self.result = source, result
        self.pair_in, self.held, self.line_in = pair_in.at[index], held.at[index], line_in.at[index]
        self.sends, self.recvs = sends.at[index], recvs.at[index]
        self.outer = lax.axis_size("row") // 2
        self.slice = PANEL // (2 * self.outer)
        me = lax.axis_index("row")
        self.side, self.along = me % 2, me // 2
        self.partner = self.along * 2 + 1 - self.side
        self.started = []

    def rows(self, side, along):
        start = side * (PANEL // 2) + along * self.slice
        return pl.ds(pl.multiple_of(start, self.slice), self.slice)

    def peer(self, offset):
        return lax.rem(self.along + offset, self.outer)

    def before(self, offset):
        return lax.rem(self.along + self.outer - offset, self.outer)

    def send(self, stage, slot, source, target, device):
        copy = pltpu.make_async_remote_copy(
            src_ref=source,
            dst_ref=target,
            send_sem=self.sends.at[stage, slot],
            recv_sem=self.recvs.at[stage, slot],
            device_id={"row": device},
            device_id_type=pl.DeviceIdType.MESH,
        )
        copy.start()
        self.started.append(copy)
        return copy

    def order(self):
        return list(range(1, self.outer)) + [0]

    def start(self):
        self.pair = {}
        for offset in self.order():
            rows = self.rows(1 - self.side, self.peer(offset))
            self.pair[offset] = self.send(
                0, offset, self.source.at[rows], self.pair_in.at[offset], self.partner
            )

    def middle(self):
        self.line = {}
        for offset in self.order():
            self.pair[offset].wait_recv()
            rows = self.rows(self.side, self.peer(offset))
            self.held[offset] = self.source[rows, :] + self.pair_in[offset]
            if offset:
                self.line[offset] = self.send(
                    1,
                    offset,
                    self.held.at[offset],
                    self.line_in.at[offset],
                    self.peer(offset) * 2 + self.side,
                )

    def finish(self):
        whole = self.held[0]
        for offset in range(1, self.outer):
            self.line[offset].wait_recv()
            whole = whole + self.line_in[offset]
        rows = self.rows(self.side, self.along)
        self.result[rows, :] = whole
        self.back = {}
        self.last = {}
        part = self.result.at[rows]
        for offset in range(1, self.outer):
            self.back[offset] = self.send(
                2, offset, part, part, self.peer(offset) * 2 + self.side
            )
        self.last[0] = self.send(3, 0, part, part, self.partner)

    def gather(self):
        for offset in range(1, self.outer):
            self.back[offset].wait_recv()
            part = self.result.at[self.rows(self.side, self.before(offset))]
            self.last[offset] = self.send(3, offset, part, part, self.partner)

    def end(self):
        for offset in range(self.outer):
            self.last[offset].wait_recv()

    def drain(self):
        for copy in self.started:
            copy.wait_send()


def chain(
    slots, upper_far, lower_far, diag, rhs_far, tail_far,
    forward_out, solution_out,
    upper, lower, rhs, tail, own, upper_inv, lower_inv, first, part2,
    y0, y1, y2, s0, s1, s2, state, held_x, c1, c2, c3, c4, pair_in, held, line_in, sends, recvs, loads,
):
    outer = lax.axis_size("row") // 2
    me = lax.axis_index("row")
    side, along = me % 2, me // 2

    def load(index, source, target):
        copy = pltpu.make_async_copy(source, target, loads.at[index])
        copy.start()
        return copy

    cols = [pl.ds(index * PANEL, PANEL) for index in range(PANELS)]
    got_tail = load(0, tail_far, tail)
    got_lower = {2: load(1, lower_far.at[:, cols[2]], lower.at[2])}
    got_upper = [load(2 + index, upper_far.at[:, cols[index]], upper.at[index]) for index in range(PANELS)]
    got_rhs = load(5, rhs_far, rhs)
    got_lower[0] = load(6, lower_far.at[:, cols[0]], lower.at[0])
    got_lower[1] = load(7, lower_far.at[:, cols[1]], lower.at[1])

    barrier = pltpu.get_barrier_semaphore()
    peers = [along * 2 + 1 - side]
    peers += [lax.rem(along + offset, outer) * 2 + side for offset in range(1, outer)]
    for peer in peers:
        pl.semaphore_signal(
            barrier, inc=1, device_id={"row": peer}, device_id_type=pl.DeviceIdType.MESH
        )
    pl.semaphore_wait(barrier, len(peers))

    block_id = slots[me]
    mine = jnp.full(rhs.shape, block_id, jnp.int32)
    mine_square = jnp.full((PANEL, PANEL), block_id, jnp.int32)
    mine_across = jnp.full((1, PANEL), block_id, jnp.int32)

    def choose(which, values):
        return jnp.where(which == 0, values[0], jnp.where(which == 1, values[1], values[2]))

    def partial(index):
        return dot3(lower[index], jnp.where(mine >= PANELS, tail[...], 0.0), TN)

    def make(index, source, result):
        return Sum(index, source, pair_in, held, line_in, result, sends, recvs)

    got_tail.wait()
    got_lower[2].wait()
    part2[...] = partial(2)
    sum_c2 = make(1, part2, s2)
    sum_c2.start()

    for copy in got_upper:
        copy.wait()
    across = choose(mine_across, [diag[:, index * PANEL : (index + 1) * PANEL] for index in range(PANELS)])
    row = lax.broadcasted_iota(jnp.int32, (TILE, TILE), 0)
    col = lax.broadcasted_iota(jnp.int32, (TILE, TILE), 1)
    down = [
        jnp.sum(jnp.where(row == col, across[:, start : start + TILE], 0.0), axis=1, keepdims=True)
        for start in range(0, PANEL, TILE)
    ]
    own[...] = choose(mine_square, upper) / jnp.concatenate(down, axis=0)

    def part(start, first_col, size):
        return own[start : start + size, first_col : first_col + size]

    stages = inverse_stages(part, PANEL)
    next(stages)
    sum_c2.middle()
    next(stages)
    upper_inv[...] = next(stages) / across
    got_rhs.wait()
    first[...] = jnp.where(mine == 0, dot3(upper_inv[...], rhs[...]), 0.0)
    sum_y0 = make(0, first, y0)
    sum_y0.start()
    got_lower[0].wait()
    got_lower[1].wait()
    own[...] = choose(mine_square, lower)
    stages = inverse_stages(part, PANEL)
    sum_c2.finish()
    next(stages)
    sum_y0.middle()
    sum_c2.gather()
    next(stages)
    sum_y0.finish()
    sum_y0.gather()
    lower_inv[...] = next(stages).T
    sum_c2.end()
    sum_y0.end()

    state[...] = rhs[...] - jnp.where(mine > 0, dot3(upper[0], y0[...]), 0.0)
    c1[...] = jnp.where(mine == 1, dot3(upper_inv[...], state[...]), 0.0)
    sum_y1 = make(2, c1, y1)
    sum_y1.start()
    c3[...] = partial(1)
    sum_y1.middle()
    c4[...] = partial(0)
    sum_y1.finish()
    sum_y1.gather()
    sum_y1.end()

    state[...] = state[...] - jnp.where(mine > 1, dot3(upper[1], y1[...]), 0.0)
    c2[...] = jnp.where(mine == 2, dot3(upper_inv[...], state[...]), 0.0)
    held_x[...] = jnp.where(mine == 2, dot3(lower_inv[...], c2[...] - s2[...]), 0.0)
    c3[...] = c3[...] + dot3(lower[1], held_x[...], TN)
    sum_c1 = make(3, c3, s1)
    sum_y2 = make(4, c2, y2)
    sum_c1.start()
    sum_y2.start()
    c4[...] = c4[...] + dot3(lower[0], held_x[...], TN)
    sum_c1.middle()
    sum_y2.middle()
    sum_c1.finish()
    sum_c1.gather()
    sum_y2.finish()
    sum_c1.end()

    x1 = jnp.where(mine == 1, dot3(lower_inv[...], y1[...] - s1[...]), 0.0)
    held_x[...] = held_x[...] + x1
    c4[...] = c4[...] + dot3(lower[0], x1, TN)
    sum_c0 = make(5, c4, s0)
    sum_c0.start()
    sum_y2.gather()
    sum_c0.middle()
    sum_y2.end()
    sum_c0.finish()
    sum_c0.gather()
    past = state[...] - dot3(upper[2], y2[...])
    forward_out[...] = jnp.where(mine >= PANELS, past, choose(mine, [y0[...], y1[...], y2[...]]))
    sum_c0.end()
    x0 = dot3(lower_inv[...], y0[...] - s0[...])
    head = jnp.where(mine == 0, x0, held_x[...])
    solution_out[...] = jnp.where(mine >= PANELS, tail[...], head)
    for one in (sum_y0, sum_c2, sum_y1, sum_c1, sum_y2, sum_c0):
        one.drain()


def body(row_count, u_panels, u_diag, l_panels, right_side, x_tail, slot_blocks):
    width = right_side.shape[1]
    square, block = (PANEL, PANEL), (PANEL, width)
    outer = row_count // 2
    piece = PANEL // row_count
    sums = 6
    vmem = pl.BlockSpec(memory_space=pltpu.VMEM)
    far = pl.BlockSpec(memory_space=pl.ANY)
    slots = pltpu.VMEM((sums, outer, piece, width), F32)
    return pl.pallas_call(
        chain,
        in_specs=[pl.BlockSpec(memory_space=pltpu.SMEM), far, far, vmem, far, far],
        out_specs=[vmem] * 2,
        out_shape=[jax.ShapeDtypeStruct(block, F32)] * 2,
        scratch_shapes=[pltpu.VMEM((PANELS, *square), F32)] * 2
        + [pltpu.VMEM(block, F32)] * 2
        + [pltpu.VMEM(square, F32)] * 3
        + [pltpu.VMEM(block, F32)] * 14
        + [slots] * 3
        + [pltpu.SemaphoreType.DMA((sums, 4, outer))] * 2
        + [pltpu.SemaphoreType.DMA((8,))],
        compiler_params=pltpu.CompilerParams(
            collective_id=0, has_side_effects=True, vmem_limit_bytes=56 * 1024 * 1024
        ),
    )(slot_blocks, u_panels, l_panels, u_diag.reshape(1, -1), right_side, x_tail)


def solution(mesh):
    placed = (
        P(("group", "row"), None),
        P("group"),
        P(("group", "row"), None),
        P(("group", "row"), "rhs"),
        P(("group", "row"), "rhs"),
        P("group"),
    )
    return jax.shard_map(
        functools.partial(body, mesh.shape["row"]),
        mesh=mesh,
        in_specs=placed,
        out_specs=(P(("group", "row"), "rhs"), P(("group", "row"), "rhs")),
        check_vma=False,
    )
```

```python
import functools

import jax
import jax.numpy as jnp
from jax import lax
from jax.experimental import pallas as pl
from jax.experimental.pallas import tpu as pltpu
from jax.sharding import PartitionSpec as P

PANEL = 512
PANELS = 3
TILE = 128
HALVES = 2
BASE = 16
F32 = jnp.float32
NN = (((1,), (0,)), ((), ()))
TN = (((0,), (0,)), ((), ()))


def split(value):
    high = value.astype(jnp.bfloat16)
    return high, (value - high.astype(F32)).astype(jnp.bfloat16)


def dot3(left, right, dims=NN):
    lh, ll = split(left)
    rh, rl = split(right)
    dot = functools.partial(lax.dot_general, dimension_numbers=dims, preferred_element_type=F32)
    wide = right.shape[1]
    if wide > TILE:
        return dot(lh, rh) + (dot(lh, rl) + dot(ll, rh))
    both = dot(lh, jnp.concatenate([rh, rl], axis=1))
    return both[:, :wide] + (both[:, wide:] + dot(ll, rh))


def inverse_stages(part, size):
    row = lax.broadcasted_iota(jnp.int32, (TILE, TILE), 0)
    col = lax.broadcasted_iota(jnp.int32, (TILE, TILE), 1)
    eye = jnp.where(row == col, 1.0, 0.0)
    done = []
    for start in range(0, size, TILE):
        tile = part(start, start, TILE)
        power = jnp.where((row // BASE == col // BASE) & (row > col), tile, 0.0)
        inverse = eye - power
        order = 2
        while order < BASE:
            power = dot3(power, power)
            inverse = inverse + dot3(inverse, power)
            order *= 2
        block = BASE
        while block < TILE:
            off = jnp.where(
                (row // (2 * block) == col // (2 * block)) & (row // block > col // block), tile, 0.0
            )
            inverse = inverse - dot3(inverse, dot3(off, inverse))
            block *= 2
        done.append(inverse)
        if start % (2 * TILE):
            yield None
    block = TILE
    while block < size:
        merged = []
        for index in range(0, len(done), 2):
            start = index * block
            off = part(start + block, start, block)
            corner = -dot3(done[index + 1], dot3(off, done[index]))
            top = jnp.concatenate([done[index], jnp.zeros_like(corner)], axis=1)
            merged.append(jnp.concatenate([top, jnp.concatenate([corner, done[index + 1]], axis=1)], axis=0))
        done = merged
        block *= 2
    yield done[0]


class Sum:
    def __init__(self, index, source, pair_in, held, line_in, result, sends, recvs):
        self.source, self.result = source, result
        self.pair_in, self.held, self.line_in = pair_in.at[index], held.at[index], line_in.at[index]
        self.sends, self.recvs = sends.at[index], recvs.at[index]
        self.outer = lax.axis_size("row") // 2
        self.slice = PANEL // (2 * self.outer)
        me = lax.axis_index("row")
        self.side, self.along = me % 2, me // 2
        self.partner = self.along * 2 + 1 - self.side
        self.started = []

    def rows(self, side, along):
        start = side * (PANEL // 2) + along * self.slice
        return pl.ds(pl.multiple_of(start, self.slice), self.slice)

    def peer(self, offset):
        return lax.rem(self.along + offset, self.outer)

    def before(self, offset):
        return lax.rem(self.along + self.outer - offset, self.outer)

    def send(self, stage, slot, source, target, device):
        copy = pltpu.make_async_remote_copy(
            src_ref=source,
            dst_ref=target,
            send_sem=self.sends.at[stage, slot],
            recv_sem=self.recvs.at[stage, slot],
            device_id={"row": device},
            device_id_type=pl.DeviceIdType.MESH,
        )
        copy.start()
        self.started.append(copy)
        return copy

    def order(self):
        return list(range(1, self.outer)) + [0]

    def start(self):
        self.pair = {}
        for offset in self.order():
            rows = self.rows(1 - self.side, self.peer(offset))
            self.pair[offset] = self.send(
                0, offset, self.source.at[rows], self.pair_in.at[offset], self.partner
            )

    def middle(self):
        self.line = {}
        for offset in self.order():
            self.pair[offset].wait_recv()
            rows = self.rows(self.side, self.peer(offset))
            self.held[offset] = self.source[rows, :] + self.pair_in[offset]
            if offset:
                self.line[offset] = self.send(
                    1,
                    offset,
                    self.held.at[offset],
                    self.line_in.at[offset],
                    self.peer(offset) * 2 + self.side,
                )

    def finish(self):
        whole = self.held[0]
        for offset in range(1, self.outer):
            self.line[offset].wait_recv()
            whole = whole + self.line_in[offset]
        rows = self.rows(self.side, self.along)
        self.result[rows, :] = whole
        self.back = {}
        self.last = {}
        part = self.result.at[rows]
        for offset in range(1, self.outer):
            self.back[offset] = self.send(
                2, offset, part, part, self.peer(offset) * 2 + self.side
            )
        self.last[0] = self.send(3, 0, part, part, self.partner)

    def gather(self):
        for offset in range(1, self.outer):
            self.back[offset].wait_recv()
            part = self.result.at[self.rows(self.side, self.before(offset))]
            self.last[offset] = self.send(3, offset, part, part, self.partner)

    def end(self):
        for offset in range(self.outer):
            self.last[offset].wait_recv()

    def drain(self):
        for copy in self.started:
            copy.wait_send()


def chain(
    slots, upper_far, lower_far, diag, rhs_far, tail_far,
    forward_out, solution_out,
    upper, lower, rhs, tail, own, upper_inv, lower_inv, first, part2,
    y0, y1, y2, s0, s1, s2, state, held_x, c1, c2, c3, c4, pair_in, held, line_in, sends, recvs, loads,
):
    outer = lax.axis_size("row") // 2
    me = lax.axis_index("row")
    side, along = me % 2, me // 2

    def load(index, source, target):
        copy = pltpu.make_async_copy(source, target, loads.at[index])
        copy.start()
        return copy

    cols = [pl.ds(index * PANEL, PANEL) for index in range(PANELS)]
    got_tail = load(0, tail_far, tail)
    got_lower = {2: load(1, lower_far.at[:, cols[2]], lower.at[2])}
    got_upper = [load(2 + index, upper_far.at[:, cols[index]], upper.at[index]) for index in range(PANELS)]
    got_rhs = load(5, rhs_far, rhs)
    got_lower[0] = load(6, lower_far.at[:, cols[0]], lower.at[0])
    got_lower[1] = load(7, lower_far.at[:, cols[1]], lower.at[1])

    barrier = pltpu.get_barrier_semaphore()
    peers = [along * 2 + 1 - side]
    peers += [lax.rem(along + offset, outer) * 2 + side for offset in range(1, outer)]
    for peer in peers:
        pl.semaphore_signal(
            barrier, inc=1, device_id={"row": peer}, device_id_type=pl.DeviceIdType.MESH
        )
    pl.semaphore_wait(barrier, len(peers))

    block_id = slots[me]
    half = y0.shape[-1]
    mine = jnp.full((PANEL, half), block_id, jnp.int32)
    mine_square = jnp.full((PANEL, PANEL), block_id, jnp.int32)
    mine_across = jnp.full((1, PANEL), block_id, jnp.int32)
    parts = [slice(index * half, (index + 1) * half) for index in range(HALVES)]

    def choose(which, values):
        return jnp.where(which == 0, values[0], jnp.where(which == 1, values[1], values[2]))

    def partial(index, target):
        for here, cut in enumerate(parts):
            target[here] = dot3(lower[index], jnp.where(mine >= PANELS, tail[:, cut], 0.0), TN)

    def make(index, source, result):
        return [
            Sum(
                index * HALVES + here, source.at[here], pair_in, held, line_in, result.at[here], sends, recvs
            )
            for here in range(HALVES)
        ]

    got_tail.wait()
    got_lower[2].wait()
    partial(2, part2)
    sum_y0, sum_c2, sum_y1 = make(0, first, y0), make(1, part2, s2), make(2, c1, y1)
    sum_c1, sum_y2, sum_c0 = make(3, c3, s1), make(4, c2, y2), make(5, c4, s0)
    for one in sum_c2:
        one.start()

    for copy in got_upper:
        copy.wait()
    across = choose(mine_across, [diag[:, index * PANEL : (index + 1) * PANEL] for index in range(PANELS)])
    row = lax.broadcasted_iota(jnp.int32, (TILE, TILE), 0)
    col = lax.broadcasted_iota(jnp.int32, (TILE, TILE), 1)
    down = [
        jnp.sum(jnp.where(row == col, across[:, start : start + TILE], 0.0), axis=1, keepdims=True)
        for start in range(0, PANEL, TILE)
    ]
    own[...] = choose(mine_square, upper) / jnp.concatenate(down, axis=0)

    def part(start, first_col, size):
        return own[start : start + size, first_col : first_col + size]

    stages = inverse_stages(part, PANEL)
    next(stages)
    for one in sum_c2:
        one.middle()
    next(stages)
    upper_inv[...] = next(stages) / across
    got_rhs.wait()
    for here, cut in enumerate(parts):
        first[here] = jnp.where(mine == 0, dot3(upper_inv[...], rhs[:, cut]), 0.0)
        sum_y0[here].start()
    got_lower[0].wait()
    got_lower[1].wait()
    own[...] = choose(mine_square, lower)
    stages = inverse_stages(part, PANEL)
    sum_c2[0].finish()
    sum_y0[0].middle()
    sum_c2[1].finish()
    next(stages)
    sum_y0[1].middle()
    sum_y0[0].finish()
    sum_y0[0].gather()
    next(stages)
    sum_y0[1].finish()
    sum_c2[0].gather()
    sum_c2[1].gather()
    lower_inv[...] = next(stages).T
    sum_y0[0].end()

    def second(here):
        state[here] = rhs[:, parts[here]] - jnp.where(mine > 0, dot3(upper[0], y0[here]), 0.0)
        c1[here] = jnp.where(mine == 1, dot3(upper_inv[...], state[here]), 0.0)
        sum_y1[here].start()

    def third(here):
        state[here] = state[here] - jnp.where(mine > 1, dot3(upper[1], y1[here]), 0.0)
        c2[here] = jnp.where(mine == 2, dot3(upper_inv[...], state[here]), 0.0)
        held_x[here] = jnp.where(mine == 2, dot3(lower_inv[...], c2[here] - s2[here]), 0.0)
        c3[here] = c3[here] + dot3(lower[1], held_x[here], TN)
        sum_c1[here].start()
        sum_y2[here].start()
        c4[here] = c4[here] + dot3(lower[0], held_x[here], TN)

    def fourth(here):
        x1 = jnp.where(mine == 1, dot3(lower_inv[...], y1[here] - s1[here]), 0.0)
        held_x[here] = held_x[here] + x1
        c4[here] = c4[here] + dot3(lower[0], x1, TN)
        sum_c0[here].start()

    def forward_end(here):
        sum_y2[here].end()
        past = state[here] - dot3(upper[2], y2[here])
        forward_out[:, parts[here]] = jnp.where(
            mine >= PANELS, past, choose(mine, [y0[here], y1[here], y2[here]])
        )

    def backward_end(here):
        sum_c0[here].end()
        x0 = dot3(lower_inv[...], y0[here] - s0[here])
        head = jnp.where(mine == 0, x0, held_x[here])
        solution_out[:, parts[here]] = jnp.where(mine >= PANELS, tail[:, parts[here]], head)

    second(0)
    sum_y0[1].gather()
    partial(1, c3)
    sum_y0[1].end()
    second(1)
    sum_y1[0].middle()
    partial(0, c4)
    sum_y1[0].finish()
    sum_y1[1].middle()
    sum_y1[0].gather()
    sum_y1[1].finish()
    sum_c2[0].end()
    sum_c2[1].end()
    sum_y1[0].end()
    third(0)
    sum_y1[1].gather()
    sum_c1[0].middle()
    sum_y1[1].end()
    third(1)
    sum_c1[0].finish()
    sum_c1[1].middle()
    sum_c1[0].gather()
    sum_y2[0].middle()
    sum_c1[1].finish()
    sum_y2[1].middle()
    sum_c1[0].end()
    fourth(0)
    sum_c1[1].gather()
    sum_y2[0].finish()
    sum_c0[0].middle()
    sum_c1[1].end()
    fourth(1)
    sum_y2[1].finish()
    sum_c0[0].finish()
    sum_c0[1].middle()
    sum_c0[0].gather()
    sum_y2[0].gather()
    sum_c0[1].finish()
    sum_y2[1].gather()
    sum_c0[1].gather()
    forward_end(0)
    backward_end(0)
    forward_end(1)
    backward_end(1)
    for both in (sum_y0, sum_c2, sum_y1, sum_c1, sum_y2, sum_c0):
        for one in both:
            one.drain()


def body(row_count, u_panels, u_diag, l_panels, right_side, x_tail, slot_blocks):
    width = right_side.shape[1]
    square, block = (PANEL, PANEL), (PANEL, width)
    outer = row_count // 2
    piece = PANEL // row_count
    sums = 6 * HALVES
    halves = (HALVES, PANEL, width // HALVES)
    vmem = pl.BlockSpec(memory_space=pltpu.VMEM)
    far = pl.BlockSpec(memory_space=pl.ANY)
    slots = pltpu.VMEM((sums, outer, piece, width // HALVES), F32)
    return pl.pallas_call(
        chain,
        in_specs=[pl.BlockSpec(memory_space=pltpu.SMEM), far, far, vmem, far, far],
        out_specs=[vmem] * 2,
        out_shape=[jax.ShapeDtypeStruct(block, F32)] * 2,
        scratch_shapes=[pltpu.VMEM((PANELS, *square), F32)] * 2
        + [pltpu.VMEM(block, F32)] * 2
        + [pltpu.VMEM(square, F32)] * 3
        + [pltpu.VMEM(halves, F32)] * 14
        + [slots] * 3
        + [pltpu.SemaphoreType.DMA((sums, 4, outer))] * 2
        + [pltpu.SemaphoreType.DMA((8,))],
        compiler_params=pltpu.CompilerParams(
            collective_id=0, has_side_effects=True, vmem_limit_bytes=56 * 1024 * 1024
        ),
    )(slot_blocks, u_panels, l_panels, u_diag.reshape(1, -1), right_side, x_tail)


def solution(mesh):
    placed = (
        P(("group", "row"), None),
        P("group"),
        P(("group", "row"), None),
        P(("group", "row"), "rhs"),
        P(("group", "row"), "rhs"),
        P("group"),
    )
    return jax.shard_map(
        functools.partial(body, mesh.shape["row"]),
        mesh=mesh,
        in_specs=placed,
        out_specs=(P(("group", "row"), "rhs"), P(("group", "row"), "rhs")),
        check_vma=False,
    )
```
